32 devices in a mesh: row: 8 (over z, y), col: 4 (over x, core).
Axes of the slice: x: 2, y: 2, z: 4, core: 2. Of those that a mesh axis runs over, the one named last changes fastest.
Arguments:
- coeffs: float32 [16384, 2048], P('row', 'col'), may hold values from -0.4375 to 0.4375
- pattern: int32 [256, 32], P('row', 'col'), may hold values from 0 to 1, as said below
Outputs:
- band: float32 [32, 3, 512, 512], P(('row', 'col'))
The draws below stay inside these ranges and needn't reach their ends.
Inputs may be any that keep to these rules, and one draw needn't show every extreme that they name: Orbital locality: with c = (a * 32) // 256, pattern[a, b] is 0 unless the circular distance min((b - c) mod 32, (c - b) mod 32) is at most 4. Some block row keeps a block at distance exactly 4 (where 32 allows it); no other structure is promised.
All inputs are finite; a program needn't handle non-finite values.
Results may differ from the reference program's by a relative error of at most 0.0003.
Values sent between devices are 32-bit elements; how exact they have to be, the bound alone decides.
A program may use at most 128 MiB of HBM per device.

```python
import jax
import jax.numpy as jnp
from jax import lax

BLOCK = 64
R_SUB = 512
STEPS = 3
BASIS = 16384
ORBITALS = 2048
NSUB = 32
NBR = 256
NBO = 32


def draw_pattern(key, part):
    local_key = jax.random.fold_in(key, 7)
    reach_key, keep_key, special_key = jax.random.split(local_key, 3)
    block_rows = jnp.arange(NBR, dtype=jnp.int32)
    block_cols = jnp.arange(NBO, dtype=jnp.int32)
    center = block_rows * NBO // NBR
    reach = jax.random.randint(reach_key, (NBR,), 1, 5, dtype=jnp.int32)
    special = jax.random.randint(special_key, (), 0, NBR, dtype=jnp.int32)
    reach = jnp.where(block_rows == special, 4, reach)
    offset = (block_cols[None, :] - center[:, None]) % NBO
    offset = jnp.minimum(offset, NBO - offset)
    keep = jax.random.randint(keep_key, (NBR, NBO), 0, 4, dtype=jnp.int32) < 3
    edge = block_cols[None, :] == ((center + reach) % NBO)[:, None]
    keep = jnp.logical_or(keep, edge)
    return jnp.logical_and(offset <= reach[:, None], keep).astype(jnp.int32)


def steps_of(key, extent, shards, smallest, top_value):
    factor_of, own = 1.0, jax.random.fold_in(key, 6)
    for dim, shards_of in shards:
        draws = jnp.exp(jax.random.uniform(jax.random.fold_in(own, dim), (shards_of,), jnp.float32, smallest / len(shards), top_value / len(shards)))
        factor_of = factor_of * jnp.repeat(draws, extent[dim] // shards_of).reshape([-1 if axis == dim else 1 for axis in range(len(extent))])
    return factor_of


def gaussian(own_key, shape, scale, most, pieces=(), kind=jnp.bfloat16):
    drawn = jax.random.normal(own_key, shape, jnp.float32) * scale
    if len(pieces) > 0:
        drawn = steps_of(own_key, shape, pieces, -0.22, 0.18) * drawn
    return jnp.clip(drawn, min=-most, max=most).astype(kind)


def setup_inputs(seed: int = 0) -> dict:
    splits = jax.random.split(jax.random.key(seed), 3)
    coeffs = gaussian(splits[0], (BASIS, ORBITALS), (max(ORBITALS // 12, BLOCK)) ** -0.5, 0.4375, ((0, 8), (1, 4)), jnp.float32)
    pattern = draw_pattern(jax.random.fold_in(splits[2], 71), 0)
    return dict(coeffs=coeffs, pattern=pattern)


def reference(coeffs, pattern):
    shaped = coeffs.reshape(NBR, BLOCK, NBO, BLOCK)
    masked = (shaped * pattern.astype(jnp.float32)[:, None, :, None]).reshape(NSUB, R_SUB, ORBITALS)
    offsets = jnp.arange(STEPS, dtype=jnp.int32)

    def one_block(index):
        picks = ((index + offsets) % NSUB).astype(jnp.int32)
        near = masked[picks].reshape(STEPS * R_SUB, ORBITALS)
        own = masked[index]
        product = jnp.dot(own, near.T, precision=lax.Precision.HIGHEST, preferred_element_type=jnp.float32)
        return product.reshape(R_SUB, STEPS, R_SUB).transpose(1, 0, 2)

    return lax.map(one_block, jnp.arange(NSUB, dtype=jnp.int32))
```

```python
import functools

import jax
import jax.numpy as jnp
from jax import lax
from jax.experimental import pallas as pl
from jax.experimental.pallas import tpu as pltpu
from jax.sharding import PartitionSpec as P

BLOCK = 64
STEPS = 3
REACH = 4
LANES = 128
MESH = pl.DeviceIdType.MESH


def kernel(
    nrow, ncol, nbr, nbo, coeffs_ref, pattern_ref, out_ref, stage, recv, left, right,
    load_sem, send_sem, recv_sem, pass_sem,
):
    r, k = lax.axis_index("row"), lax.axis_index("col")
    core = k % 2
    nsub = nrow * ncol
    width = stage.shape[2]
    per = coeffs_ref.shape[1] // LANES
    ntile = nbo * BLOCK // LANES
    span = recv.shape[1]
    blocks = width // BLOCK
    late = 1 if blocks * nbo == nbr else 0

    def first_tile(g):
        center = g * blocks * nbo // nbr
        return (center + nbo - REACH) // 2 % ntile

    loads = lambda l, t: pltpu.make_async_copy(
        coeffs_ref.at[pl.ds(l * width, width), pl.ds(t * LANES, LANES)], stage.at[l, t], load_sem.at[l, t]
    )
    for l in range(ncol):
        for t in range(per):
            loads(l, t).start()

    up, down = (r + 1) % nrow, (r + nrow - 1) % nrow
    barrier = pltpu.get_barrier_semaphore()
    for d in range(1, ncol):
        pl.semaphore_signal(barrier, inc=1, device_id=(r, (k + d) % ncol), device_id_type=MESH)
    for d in range(ncol):
        pl.semaphore_signal(barrier, inc=1, device_id=(up, (k + d) % ncol), device_id_type=MESH)
        pl.semaphore_signal(barrier, inc=1, device_id=(down, (k + d) % ncol), device_id_type=MESH)

    lane = lax.broadcasted_iota(jnp.int32, (1, LANES), 1)

    def mask(l, t):
        for b in range(blocks):
            p0 = pattern_ref[l * blocks + b, 2 * t].astype(jnp.float32)
            p1 = pattern_ref[l * blocks + b, 2 * t + 1].astype(jnp.float32)
            rows = pl.ds(b * BLOCK, BLOCK)
            stage[l, t, rows, :] = stage[l, t, rows, :] * jnp.where(lane < BLOCK, p0, p1)

    def target(l, t, c):
        h = l % 2 + 2 * c
        base = (r * ncol + l - h + nsub) % nsub
        j = (k * per + t - first_tile(base) + ntile) % ntile
        wanted = jnp.logical_and(j < span, j >= late * c)
        row, col = base // ncol, base % ncol + l % 2
        here = jnp.logical_and(row == r, col == k)
        j = jnp.minimum(j, span - 1)
        return h, j, row, col, jnp.logical_and(wanted, here), jnp.logical_and(wanted, jnp.logical_not(here))

    def send(l, t, c):
        h, j, row, col, local, remote = target(l, t, c)
        move = pltpu.make_async_remote_copy(
            stage.at[l, t], recv.at[h, j], send_sem.at[l, t, c], recv_sem.at[h, j],
            device_id=(row, col), device_id_type=MESH,
        )
        return local, remote, pltpu.make_async_copy(stage.at[l, t], recv.at[h, j], recv_sem.at[h, j]), move

    def mask_all(l, carry):
        for t in range(per):
            loads(l, t).wait()
            mask(l, t)
        return carry

    lax.fori_loop(0, ncol, mask_all, 0)
    pl.semaphore_wait(barrier, 3 * ncol - 1)

    def send_all(l, carry):
        for t in range(per):
            for c in range(2):
                local, remote, own, move = send(l, t, c)
                pl.when(local)(own.start)
                pl.when(remote)(move.start)
        return carry

    lax.fori_loop(0, ncol, send_all, 0)
    out_ref[...] = jnp.zeros_like(out_ref)

    def pass_on(h, j):
        return pltpu.make_async_remote_copy(
            recv.at[h, j], recv.at[h, j], pass_sem.at[j], recv_sem.at[h, j],
            device_id=(r, k + 1 - 2 * core), device_id_type=MESH,
        )

    shared, alone = 2 - core, 3 * core

    def arrived(h, j):
        pl.when(j >= jnp.where(h < 2, 0, late))(pass_on(h, j).wait_recv)

    def multiply(j, carry):
        has_shared = j >= jnp.where(shared < 2, 0, late)
        arrived(shared, j)
        pl.when(has_shared)(pass_on(shared, j).start)
        arrived(alone, j)
        arrived(1 + core, j)
        for step in range(STEPS):
            h = core + step

            @pl.when(j >= jnp.where(h < 2, 0, late))
            def _():
                x = recv[h, j]
                high = x.astype(jnp.bfloat16)
                low = (x - high.astype(jnp.float32)).astype(jnp.bfloat16)
                if step == 0:
                    left[:, 0:LANES] = high
                    left[:, LANES:2 * LANES] = low
                    left[:, 2 * LANES:3 * LANES] = high
                right[:, 0:LANES] = high
                right[:, LANES:2 * LANES] = high
                right[:, 2 * LANES:3 * LANES] = low

                def part(i, carry):
                    rows = pl.ds(pl.multiple_of(i * LANES, LANES), LANES)
                    out_ref[0, step, rows, :] += lax.dot_general(
                        left[rows, :], right[...], (((1,), (1,)), ((), ())),
                        preferred_element_type=jnp.float32,
                    )
                    return carry

                lax.fori_loop(0, width // LANES, part, 0)

        return carry

    lax.fori_loop(0, span, multiply, 0)

    def sent_all(l, carry):
        for t in range(per):
            for c in range(2):
                _, remote, _, move = send(l, t, c)
                pl.when(remote)(move.wait_send)
        return carry

    lax.fori_loop(0, ncol, sent_all, 0)

    def passed_all(j, carry):
        pl.when(j >= jnp.where(shared < 2, 0, late))(pass_on(shared, j).wait_send)
        return carry

    lax.fori_loop(0, span, passed_all, 0)


def shards(nrow, ncol, coeffs, pattern):
    rows, cols = coeffs.shape
    width = rows // ncol
    nbr, nbo = pattern.shape[0] * nrow, pattern.shape[1] * ncol
    per = cols // LANES
    span = REACH + 1
    return pl.pallas_call(
        functools.partial(kernel, nrow, ncol, nbr, nbo),
        out_shape=jax.ShapeDtypeStruct((1, STEPS, width, width), jnp.float32),
        in_specs=[pl.BlockSpec(memory_space=pl.ANY), pl.BlockSpec(memory_space=pltpu.SMEM)],
        out_specs=pl.BlockSpec(memory_space=pltpu.VMEM),
        scratch_shapes=[
            pltpu.VMEM((ncol, per, width, LANES), jnp.float32),
            pltpu.VMEM((4, span, width, LANES), jnp.float32),
            pltpu.VMEM((width, 3 * LANES), jnp.bfloat16),
            pltpu.VMEM((width, 3 * LANES), jnp.bfloat16),
            pltpu.SemaphoreType.DMA((ncol, per)),
            pltpu.SemaphoreType.DMA((ncol, per, 2)),
            pltpu.SemaphoreType.DMA((4, span)),
            pltpu.SemaphoreType.DMA((span,)),
        ],
        compiler_params=pltpu.CompilerParams(
            collective_id=0, has_side_effects=True, vmem_limit_bytes=40 << 20
        ),
        cost_estimate=pl.CostEstimate(
            flops=2 * 3 * STEPS * width * width * span * LANES,
            bytes_accessed=4 * (rows * cols + STEPS * width * width), transcendentals=0,
        ),
    )(coeffs, pattern)


def solution(mesh):
    in_specs = (P("row", "col"), P("row", "col"))
    out_specs = P(("row", "col"), None, None, None)
    body = functools.partial(shards, mesh.shape["row"], mesh.shape["col"])
    return jax.shard_map(body, mesh=mesh, in_specs=in_specs, out_specs=out_specs, check_vma=False)
```

```python
import collections
import functools

import jax
import jax.numpy as jnp
from jax import lax
from jax.experimental import pallas as pl
from jax.experimental.pallas import tpu as pltpu
from jax.sharding import PartitionSpec as P

BLOCK = 64
STEPS = 3
REACH = 4
LANES = 128
MESH = pl.DeviceIdType.MESH


def legs(a, b):
    out, at = [], list(a)
    for axis in (2, 0, 1):
        while at[axis] != b[axis]:
            step = 1 if b[axis] > at[axis] else -1
            out.append((tuple(at), axis, step))
            at[axis] += step
    return out


def planned(nrow, ncol, per, width, nbr, nbo, span, late):
    nsub, ntile, blocks = nrow * ncol, nbo * BLOCK // LANES, width // BLOCK
    place = lambda row, col: (col // 2, row % 2, row // 2)
    chips = [(x, y, z) for z in range(nrow // 2) for y in range(2) for x in range(ncol // 2)]
    tiles = []
    for g in range(nsub):
        for k in range(ncol):
            for t in range(per):
                for c in range(2):
                    l = g % ncol
                    h = l % 2 + 2 * c
                    base = (g - h) % nsub
                    first = (base * blocks * nbo // nbr + nbo - REACH) // 2 % ntile
                    j = (k * per + t - first) % ntile
                    if late * c <= j < span:
                        tiles.append((g // ncol, k, l, t, h, j, base // ncol, base % ncol + l % 2))
    load, choices, chosen = collections.Counter(), [], []
    for row, k, l, t, h, j, to_row, to_col in tiles:
        a, b = place(row, k), place(to_row, to_col)
        ways = [(None, legs(a, b))]
        for q in chips:
            if a != b and q != a and q != b and len(legs(a, q)) + len(legs(q, b)) <= 6:
                ways.append((q, legs(a, q) + legs(q, b)))
        choices.append(ways)
        chosen.append(0)
        load.update(ways[0][1])
    for _ in range(12):
        for i, ways in enumerate(choices):
            load.subtract(ways[chosen[i]][1])
            costs = [
                (sum((load[e] + 1) ** 6 - load[e] ** 6 for e in way) + (0 if q is None else 72900), n != chosen[i], n)
                for n, (q, way) in enumerate(ways)
            ]
            chosen[i] = min(costs)[2]
            load.update(ways[chosen[i]][1])
    sends = collections.defaultdict(list)
    relays = collections.defaultdict(list)
    used = collections.Counter()
    order = sorted(range(len(tiles)), key=lambda i: (chosen[i] == 0, tiles[i][5], i))
    for i in order:
        row, k, l, t, h, j, to_row, to_col = tiles[i]
        q = choices[i][chosen[i]][0]
        if q is None:
            sends[row, k].append((l, t, h, j, to_row, to_col, None))
        else:
            via_row, via_col = q[2] * 2 + q[1], q[0] * 2 + used[q] % 2
            used[q] += 1
            slot = len(relays[via_row, via_col])
            sends[row, k].append((l, t, h, j, via_row, via_col, slot))
            relays[via_row, via_col].append((h, j, to_row, to_col))
    peers = collections.defaultdict(set)
    for row in range(nrow):
        for k in range(0, ncol, 2):
            peers[row, k].add((row, k + 1))
            peers[row, k + 1].add((row, k))
    for a in list(sends):
        for move in sends[a]:
            if move[4:6] != a:
                peers[a].add(move[4:6])
                peers[move[4:6]].add(a)
    for a in list(relays):
        for move in relays[a]:
            peers[a].add(move[2:4])
            peers[move[2:4]].add(a)
    return sends, relays, peers


def kernel(
    nrow, ncol, nbr, nbo, plan, coeffs_ref, pattern_ref, out_ref, stage, recv, hold, left, right,
    load_sem, send_sem, recv_sem, pass_sem, via_sem, hold_sem,
):
    r, k = lax.axis_index("row"), lax.axis_index("col")
    core = k % 2
    nsub = nrow * ncol
    width = stage.shape[2]
    per = coeffs_ref.shape[1] // LANES
    ntile = nbo * BLOCK // LANES
    span = recv.shape[1]
    blocks = width // BLOCK
    late = 1 if blocks * nbo == nbr else 0

    def first_tile(g):
        center = g * blocks * nbo // nbr
        return (center + nbo - REACH) // 2 % ntile

    loads = lambda l, t: pltpu.make_async_copy(
        coeffs_ref.at[pl.ds(l * width, width), pl.ds(t * LANES, LANES)], stage.at[l, t], load_sem.at[l, t]
    )
    for l in range(ncol):
        for t in range(per):
            loads(l, t).start()

    barrier = pltpu.get_barrier_semaphore()
    me = r * ncol + k
    if plan is None:
        up, down = (r + 1) % nrow, (r + nrow - 1) % nrow
        for d in range(1, ncol):
            pl.semaphore_signal(barrier, inc=1, device_id=(r, (k + d) % ncol), device_id_type=MESH)
        for d in range(ncol):
            pl.semaphore_signal(barrier, inc=1, device_id=(up, (k + d) % ncol), device_id_type=MESH)
            pl.semaphore_signal(barrier, inc=1, device_id=(down, (k + d) % ncol), device_id_type=MESH)
    else:
        sends, relays, peers = plan
        for row, col in sorted(peers):

            @pl.when(me == row * ncol + col)
            def _(others=sorted(peers[row, col])):
                for other in others:
                    pl.semaphore_signal(barrier, inc=1, device_id=other, device_id_type=MESH)

    lane = lax.broadcasted_iota(jnp.int32, (1, LANES), 1)

    def mask(l, t):
        for b in range(blocks):
            p0 = pattern_ref[2 * t, l * blocks + b].astype(jnp.float32)
            p1 = pattern_ref[2 * t + 1, l * blocks + b].astype(jnp.float32)
            rows = pl.ds(b * BLOCK, BLOCK)
            stage[l, t, rows, :] = stage[l, t, rows, :] * jnp.where(lane < BLOCK, p0, p1)

    def target(l, t, c):
        h = l % 2 + 2 * c
        base = (r * ncol + l - h + nsub) % nsub
        j = (k * per + t - first_tile(base) + ntile) % ntile
        wanted = jnp.logical_and(j < span, j >= late * c)
        row, col = base // ncol, base % ncol + l % 2
        here = jnp.logical_and(row == r, col == k)
        j = jnp.minimum(j, span - 1)
        return h, j, row, col, jnp.logical_and(wanted, here), jnp.logical_and(wanted, jnp.logical_not(here))

    def send(l, t, c):
        h, j, row, col, local, remote = target(l, t, c)
        move = pltpu.make_async_remote_copy(
            stage.at[l, t], recv.at[h, j], send_sem.at[l, t, c], recv_sem.at[h, j],
            device_id=(row, col), device_id_type=MESH,
        )
        return local, remote, pltpu.make_async_copy(stage.at[l, t], recv.at[h, j], recv_sem.at[h, j]), move

    def mask_all(l, carry):
        for t in range(per):
            loads(l, t).wait()
            mask(l, t)
        return carry

    lax.fori_loop(0, ncol, mask_all, 0)
    if plan is None:
        pl.semaphore_wait(barrier, 3 * ncol - 1)

    def send_all(l, carry):
        for t in range(per):
            for c in range(2):
                local, remote, own, move = send(l, t, c)
                pl.when(local)(own.start)
                pl.when(remote)(move.start)
        return carry

    def routed(row, col, n):
        l, t, h, j, to_row, to_col, slot = sends[row, col][n]
        if (to_row, to_col) == (row, col):
            return pltpu.make_async_copy(stage.at[l, t], recv.at[h, j], recv_sem.at[h, j])
        return pltpu.make_async_remote_copy(
            stage.at[l, t], recv.at[h, j] if slot is None else hold.at[slot], send_sem.at[l, t, h // 2],
            recv_sem.at[h, j] if slot is None else hold_sem.at[slot],
            device_id=(to_row, to_col), device_id_type=MESH,
        )

    def relayed(row, col, slot):
        h, j, to_row, to_col = relays[row, col][slot]
        return pltpu.make_async_remote_copy(
            hold.at[slot], recv.at[h, j], via_sem.at[slot], recv_sem.at[h, j],
            device_id=(to_row, to_col), device_id_type=MESH,
        )

    def taken(slot):
        return pltpu.make_async_remote_copy(
            hold.at[slot], hold.at[slot], via_sem.at[slot], hold_sem.at[slot],
            device_id=(r, k + 1 - 2 * core), device_id_type=MESH,
        )

    if plan is None:
        lax.fori_loop(0, ncol, send_all, 0)
    else:
        for row, col in sorted(peers):

            @pl.when(me == row * ncol + col)
            def _(row=row, col=col):
                pl.semaphore_wait(barrier, len(peers[row, col]))
                for n in range(len(sends.get((row, col), ()))):
                    routed(row, col, n).start()

    out_ref[...] = jnp.zeros_like(out_ref)
    if plan is not None:
        for row, col in sorted(relays):

            @pl.when(me == row * ncol + col)
            def _(row=row, col=col):
                for slot in range(len(relays[row, col])):
                    taken(slot).wait_recv()
                    relayed(row, col, slot).start()


    def pass_on(h, j):
        return pltpu.make_async_remote_copy(
            recv.at[h, j], recv.at[h, j], pass_sem.at[j], recv_sem.at[h, j],
            device_id=(r, k + 1 - 2 * core), device_id_type=MESH,
        )

    shared, alone = 2 - core, 3 * core

    def arrived(h, j):
        pl.when(j >= jnp.where(h < 2, 0, late))(pass_on(h, j).wait_recv)

    def multiply(j, carry):
        has_shared = j >= jnp.where(shared < 2, 0, late)
        arrived(shared, j)
        pl.when(has_shared)(pass_on(shared, j).start)
        arrived(alone, j)
        arrived(1 + core, j)
        for step in range(STEPS):
            h = core + step

            @pl.when(j >= jnp.where(h < 2, 0, late))
            def _():
                x = recv[h, j]
                high = x.astype(jnp.bfloat16)
                low = (x - high.astype(jnp.float32)).astype(jnp.bfloat16)
                if step == 0:
                    left[:, 0:LANES] = high
                    left[:, LANES:2 * LANES] = low
                    left[:, 2 * LANES:3 * LANES] = high
                right[:, 0:LANES] = high
                right[:, LANES:2 * LANES] = high
                right[:, 2 * LANES:3 * LANES] = low

                def part(i, carry):
                    rows = pl.ds(pl.multiple_of(i * LANES, LANES), LANES)
                    out_ref[0, step, rows, :] += lax.dot_general(
                        left[rows, :], right[...], (((1,), (1,)), ((), ())),
                        preferred_element_type=jnp.float32,
                    )
                    return carry

                lax.fori_loop(0, width // LANES, part, 0)

        return carry

    lax.fori_loop(0, span, multiply, 0)

    def sent_all(l, carry):
        for t in range(per):
            for c in range(2):
                _, remote, _, move = send(l, t, c)
                pl.when(remote)(move.wait_send)
        return carry

    if plan is None:
        lax.fori_loop(0, ncol, sent_all, 0)
    else:
        for row, col in sorted(peers):

            @pl.when(me == row * ncol + col)
            def _(row=row, col=col):
                for n, move in enumerate(sends.get((row, col), ())):
                    if move[4:6] != (row, col):
                        routed(row, col, n).wait_send()
                for slot in range(len(relays.get((row, col), ()))):
                    relayed(row, col, slot).wait_send()


    def passed_all(j, carry):
        pl.when(j >= jnp.where(shared < 2, 0, late))(pass_on(shared, j).wait_send)
        return carry

    lax.fori_loop(0, span, passed_all, 0)


def shards(nrow, ncol, coeffs, pattern):
    rows, cols = coeffs.shape
    width = rows // ncol
    nbr, nbo = pattern.shape[0] * nrow, pattern.shape[1] * ncol
    per = cols // LANES
    span = REACH + 1
    plan, held = None, 1
    if (nrow, ncol) == (8, 4):
        plan = planned(nrow, ncol, per, width, nbr, nbo, span, 1 if width // BLOCK * nbo == nbr else 0)
        held = max([1] + [len(moves) for moves in plan[1].values()])
    return pl.pallas_call(
        functools.partial(kernel, nrow, ncol, nbr, nbo, plan),
        out_shape=jax.ShapeDtypeStruct((1, STEPS, width, width), jnp.float32),
        in_specs=[pl.BlockSpec(memory_space=pltpu.HBM), pl.BlockSpec(memory_space=pltpu.SMEM)],
        out_specs=pl.BlockSpec(memory_space=pltpu.VMEM),
        scratch_shapes=[
            pltpu.VMEM((ncol, per, width, LANES), jnp.float32),
            pltpu.VMEM((4, span, width, LANES), jnp.float32),
            pltpu.VMEM((held, width, LANES), jnp.float32),
            pltpu.VMEM((width, 3 * LANES), jnp.bfloat16),
            pltpu.VMEM((width, 3 * LANES), jnp.bfloat16),
            pltpu.SemaphoreType.DMA((ncol, per)),
            pltpu.SemaphoreType.DMA((ncol, per, 2)),
            pltpu.SemaphoreType.DMA((4, span)),
            pltpu.SemaphoreType.DMA((span,)),
            pltpu.SemaphoreType.DMA((held,)),
            pltpu.SemaphoreType.DMA((held,)),
        ],
        compiler_params=pltpu.CompilerParams(
            collective_id=0, has_side_effects=True, vmem_limit_bytes=40 << 20
        ),
        cost_estimate=pl.CostEstimate(
            flops=2 * 3 * STEPS * width * width * span * LANES,
            bytes_accessed=4 * (rows * cols + STEPS * width * width), transcendentals=0,
        ),
    )(coeffs, pattern.T)


def solution(mesh):
    in_specs = (P("row", "col"), P("row", "col"))
    out_specs = P(("row", "col"), None, None, None)
    body = functools.partial(shards, mesh.shape["row"], mesh.shape["col"])
    return jax.shard_map(body, mesh=mesh, in_specs=in_specs, out_specs=out_specs, check_vma=False)
```

```python
import collections
import functools

import jax
import jax.numpy as jnp
from jax import lax
from jax.experimental import pallas as pl
from jax.experimental.pallas import tpu as pltpu
from jax.sharding import PartitionSpec as P

BLOCK = 64
STEPS = 3
REACH = 4
LANES = 128
MESH = pl.DeviceIdType.MESH


def legs(a, b):
    out, at = [], list(a)
    for axis in (2, 0, 1):
        while at[axis] != b[axis]:
            step = 1 if b[axis] > at[axis] else -1
            out.append((tuple(at), axis, step))
            at[axis] += step
    return out


def planned(nrow, ncol, per, width, nbr, nbo, span, late):
    nsub, ntile, blocks = nrow * ncol, nbo * BLOCK // LANES, width // BLOCK
    place = lambda row, col: (col // 2, row % 2, row // 2)
    chips = [(x, y, z) for z in range(nrow // 2) for y in range(2) for x in range(ncol // 2)]
    tiles = []
    for g in range(nsub):
        for k in range(ncol):
            for t in range(per):
                for c in range(2):
                    l = g % ncol
                    h = l % 2 + 2 * c
                    base = (g - h) % nsub
                    first = (base * blocks * nbo // nbr + nbo - REACH) // 2 % ntile
                    j = (k * per + t - first) % ntile
                    if late * c <= j < span:
                        tiles.append((g // ncol, k, l, t, h, j, base // ncol, base % ncol + l % 2))
    load, choices, chosen = collections.Counter(), [], []
    for row, k, l, t, h, j, to_row, to_col in tiles:
        a, b = place(row, k), place(to_row, to_col)
        ways = [(None, legs(a, b))]
        for q in chips:
            if a != b and q != a and q != b and len(legs(a, q)) + len(legs(q, b)) <= 6:
                ways.append((q, legs(a, q) + legs(q, b)))
        choices.append(ways)
        chosen.append(0)
        load.update(ways[0][1])
    for _ in range(12):
        for i, ways in enumerate(choices):
            load.subtract(ways[chosen[i]][1])
            costs = [
                (sum((load[e] + 1) ** 6 - load[e] ** 6 for e in way) + (0 if q is None else 72900), n != chosen[i], n)
                for n, (q, way) in enumerate(ways)
            ]
            chosen[i] = min(costs)[2]
            load.update(ways[chosen[i]][1])
    sends = collections.defaultdict(list)
    relays = collections.defaultdict(list)
    used = collections.Counter()
    order = sorted(range(len(tiles)), key=lambda i: (chosen[i] == 0, tiles[i][5], i))
    for i in order:
        row, k, l, t, h, j, to_row, to_col = tiles[i]
        q = choices[i][chosen[i]][0]
        if q is None:
            sends[row, k].append((l, t, h, j, to_row, to_col, None))
        else:
            via_row, via_col = q[2] * 2 + q[1], q[0] * 2 + used[q] % 2
            used[q] += 1
            slot = len(relays[via_row, via_col])
            sends[row, k].append((l, t, h, j, via_row, via_col, slot))
            relays[via_row, via_col].append((h, j, to_row, to_col))
    peers = collections.defaultdict(set)
    for row in range(nrow):
        for k in range(0, ncol, 2):
            peers[row, k].add((row, k + 1))
            peers[row, k + 1].add((row, k))
    for a in list(sends):
        for move in sends[a]:
            if move[4:6] != a:
                peers[a].add(move[4:6])
                peers[move[4:6]].add(a)
    for a in list(relays):
        for move in relays[a]:
            peers[a].add(move[2:4])
            peers[move[2:4]].add(a)
    return sends, relays, peers


def kernel(
    nrow, ncol, nbr, nbo, plan, coeffs_ref, pattern_ref, out_ref, stage, recv, hold, left, right,
    load_sem, send_sem, recv_sem, pass_sem, via_sem, hold_sem,
):
    r, k = lax.axis_index("row"), lax.axis_index("col")
    core = k % 2
    nsub = nrow * ncol
    width = stage.shape[2]
    per = coeffs_ref.shape[1] // LANES
    ntile = nbo * BLOCK // LANES
    span = recv.shape[1]
    blocks = width // BLOCK
    late = 1 if blocks * nbo == nbr else 0

    def first_tile(g):
        center = g * blocks * nbo // nbr
        return (center + nbo - REACH) // 2 % ntile

    loads = lambda l, t: pltpu.make_async_copy(
        coeffs_ref.at[pl.ds(l * width, width), pl.ds(t * LANES, LANES)], stage.at[l, t], load_sem.at[l, t]
    )
    for l in range(ncol):
        for t in range(per):
            loads(l, t).start()

    barrier = pltpu.get_barrier_semaphore()
    me = r * ncol + k
    if plan is None:
        up, down = (r + 1) % nrow, (r + nrow - 1) % nrow
        for d in range(1, ncol):
            pl.semaphore_signal(barrier, inc=1, device_id=(r, (k + d) % ncol), device_id_type=MESH)
        for d in range(ncol):
            pl.semaphore_signal(barrier, inc=1, device_id=(up, (k + d) % ncol), device_id_type=MESH)
            pl.semaphore_signal(barrier, inc=1, device_id=(down, (k + d) % ncol), device_id_type=MESH)
    else:
        sends, relays, peers = plan
        for row, col in sorted(peers):

            @pl.when(me == row * ncol + col)
            def _(others=sorted(peers[row, col])):
                for other in others:
                    pl.semaphore_signal(barrier, inc=1, device_id=other, device_id_type=MESH)

    lane = lax.broadcasted_iota(jnp.int32, (1, LANES), 1)

    def mask(l, t):
        for b in range(blocks):
            p0 = pattern_ref[2 * t, l * blocks + b].astype(jnp.float32)
            p1 = pattern_ref[2 * t + 1, l * blocks + b].astype(jnp.float32)
            rows = pl.ds(b * BLOCK, BLOCK)
            stage[l, t, rows, :] = stage[l, t, rows, :] * jnp.where(lane < BLOCK, p0, p1)

    def target(l, t, c):
        h = l % 2 + 2 * c
        base = (r * ncol + l - h + nsub) % nsub
        j = (k * per + t - first_tile(base) + ntile) % ntile
        wanted = jnp.logical_and(j < span, j >= late * c)
        row, col = base // ncol, base % ncol + l % 2
        here = jnp.logical_and(row == r, col == k)
        j = jnp.minimum(j, span - 1)
        return h, j, row, col, jnp.logical_and(wanted, here), jnp.logical_and(wanted, jnp.logical_not(here))

    def send(l, t, c):
        h, j, row, col, local, remote = target(l, t, c)
        move = pltpu.make_async_remote_copy(
            stage.at[l, t], recv.at[h, j], send_sem.at[l, t, c], recv_sem.at[h, j],
            device_id=(row, col), device_id_type=MESH,
        )
        return local, remote, pltpu.make_async_copy(stage.at[l, t], recv.at[h, j], recv_sem.at[h, j]), move

    def mask_all(l, carry):
        for t in range(per):
            loads(l, t).wait()
            mask(l, t)
        return carry

    lax.fori_loop(0, ncol, mask_all, 0)
    if plan is None:
        pl.semaphore_wait(barrier, 3 * ncol - 1)

    def send_all(l, carry):
        for t in range(per):
            for c in range(2):
                local, remote, own, move = send(l, t, c)
                pl.when(local)(own.start)
                pl.when(remote)(move.start)
        return carry

    def routed(row, col, n):
        l, t, h, j, to_row, to_col, slot = sends[row, col][n]
        if (to_row, to_col) == (row, col):
            return pltpu.make_async_copy(stage.at[l, t], recv.at[h, j], recv_sem.at[h, j])
        return pltpu.make_async_remote_copy(
            stage.at[l, t], recv.at[h, j] if slot is None else hold.at[slot], send_sem.at[l, t, h // 2],
            recv_sem.at[h, j] if slot is None else hold_sem.at[slot],
            device_id=(to_row, to_col), device_id_type=MESH,
        )

    def relayed(row, col, slot):
        h, j, to_row, to_col = relays[row, col][slot]
        return pltpu.make_async_remote_copy(
            hold.at[slot], recv.at[h, j], via_sem.at[slot], recv_sem.at[h, j],
            device_id=(to_row, to_col), device_id_type=MESH,
        )

    def taken(slot):
        return pltpu.make_async_remote_copy(
            hold.at[slot], hold.at[slot], via_sem.at[slot], hold_sem.at[slot],
            device_id=(r, k + 1 - 2 * core), device_id_type=MESH,
        )

    if plan is None:
        lax.fori_loop(0, ncol, send_all, 0)
    else:
        for row, col in sorted(peers):

            @pl.when(me == row * ncol + col)
            def _(row=row, col=col):
                pl.semaphore_wait(barrier, len(peers[row, col]))
                for n in range(len(sends.get((row, col), ()))):
                    routed(row, col, n).start()

    out_ref[...] = jnp.zeros_like(out_ref)
    if plan is not None:
        for row, col in sorted(relays):

            @pl.when(me == row * ncol + col)
            def _(row=row, col=col):
                for slot in range(len(relays[row, col])):
                    taken(slot).wait_recv()
                    relayed(row, col, slot).start()


    def pass_on(h, j):
        return pltpu.make_async_remote_copy(
            recv.at[h, j], recv.at[h, j], pass_sem.at[j], recv_sem.at[h, j],
            device_id=(r, k + 1 - 2 * core), device_id_type=MESH,
        )

    shared, alone = 2 - core, 3 * core

    def arrived(h, j):
        pl.when(j >= jnp.where(h < 2, 0, late))(pass_on(h, j).wait_recv)

    def multiply(j, carry):
        has_shared = j >= jnp.where(shared < 2, 0, late)
        arrived(shared, j)
        pl.when(has_shared)(pass_on(shared, j).start)
        arrived(alone, j)
        arrived(1 + core, j)
        for step in range(STEPS):
            h = core + step

            @pl.when(j >= jnp.where(h < 2, 0, late))
            def _():
                x = recv[h, j]
                high = x.astype(jnp.bfloat16)
                low = (x - high.astype(jnp.float32)).astype(jnp.bfloat16)
                if step == 0:
                    left[:, 0:LANES] = high
                    left[:, LANES:2 * LANES] = low
                    left[:, 2 * LANES:3 * LANES] = high
                right[:, 0:LANES] = high
                right[:, LANES:2 * LANES] = high
                right[:, 2 * LANES:3 * LANES] = low

                for i in range(2):
                    cols = pl.ds(i * (width // 2), width // 2)
                    out_ref[0, step, :, cols] += lax.dot_general(
                        left[...], right[cols, :], (((1,), (1,)), ((), ())),
                        preferred_element_type=jnp.float32,
                    )

        return carry

    lax.fori_loop(0, span, multiply, 0)

    def sent_all(l, carry):
        for t in range(per):
            for c in range(2):
                _, remote, _, move = send(l, t, c)
                pl.when(remote)(move.wait_send)
        return carry

    if plan is None:
        lax.fori_loop(0, ncol, sent_all, 0)
    else:
        for row, col in sorted(peers):

            @pl.when(me == row * ncol + col)
            def _(row=row, col=col):
                for n, move in enumerate(sends.get((row, col), ())):
                    if move[4:6] != (row, col):
                        routed(row, col, n).wait_send()
                for slot in range(len(relays.get((row, col), ()))):
                    relayed(row, col, slot).wait_send()


    def passed_all(j, carry):
        pl.when(j >= jnp.where(shared < 2, 0, late))(pass_on(shared, j).wait_send)
        return carry

    lax.fori_loop(0, span, passed_all, 0)


def shards(nrow, ncol, coeffs, pattern):
    rows, cols = coeffs.shape
    width = rows // ncol
    nbr, nbo = pattern.shape[0] * nrow, pattern.shape[1] * ncol
    per = cols // LANES
    span = REACH + 1
    plan, held = None, 1
    if (nrow, ncol) == (8, 4):
        plan = planned(nrow, ncol, per, width, nbr, nbo, span, 1 if width // BLOCK * nbo == nbr else 0)
        held = max([1] + [len(moves) for moves in plan[1].values()])
    return pl.pallas_call(
        functools.partial(kernel, nrow, ncol, nbr, nbo, plan),
        out_shape=jax.ShapeDtypeStruct((1, STEPS, width, width), jnp.float32),
        in_specs=[pl.BlockSpec(memory_space=pltpu.HBM), pl.BlockSpec(memory_space=pltpu.SMEM)],
        out_specs=pl.BlockSpec(memory_space=pltpu.VMEM),
        scratch_shapes=[
            pltpu.VMEM((ncol, per, width, LANES), jnp.float32),
            pltpu.VMEM((4, span, width, LANES), jnp.float32),
            pltpu.VMEM((held, width, LANES), jnp.float32),
            pltpu.VMEM((width, 3 * LANES), jnp.bfloat16),
            pltpu.VMEM((width, 3 * LANES), jnp.bfloat16),
            pltpu.SemaphoreType.DMA((ncol, per)),
            pltpu.SemaphoreType.DMA((ncol, per, 2)),
            pltpu.SemaphoreType.DMA((4, span)),
            pltpu.SemaphoreType.DMA((span,)),
            pltpu.SemaphoreType.DMA((held,)),
            pltpu.SemaphoreType.DMA((held,)),
        ],
        compiler_params=pltpu.CompilerParams(
            collective_id=0, has_side_effects=True, vmem_limit_bytes=40 << 20
        ),
        cost_estimate=pl.CostEstimate(
            flops=2 * 3 * STEPS * width * width * span * LANES,
            bytes_accessed=4 * (rows * cols + STEPS * width * width), transcendentals=0,
        ),
    )(coeffs, pattern.T)


def solution(mesh):
    in_specs = (P("row", "col"), P("row", "col"))
    out_specs = P(("row", "col"), None, None, None)
    body = functools.partial(shards, mesh.shape["row"], mesh.shape["col"])
    return jax.shard_map(body, mesh=mesh, in_specs=in_specs, out_specs=out_specs, check_vma=False)
```

```python
import collections
import functools

import jax
import jax.numpy as jnp
from jax import lax
from jax.experimental import pallas as pl
from jax.experimental.pallas import tpu as pltpu
from jax.sharding import PartitionSpec as P

BLOCK = 64
STEPS = 3
REACH = 4
LANES = 128
MESH = pl.DeviceIdType.MESH


def legs(a, b):
    out, at = [], list(a)
    for axis in (2, 0, 1):
        while at[axis] != b[axis]:
            step = 1 if b[axis] > at[axis] else -1
            out.append((tuple(at), axis, step))
            at[axis] += step
    return out


def planned(nrow, ncol, per, width, nbr, nbo, span, late):
    nsub, ntile, blocks = nrow * ncol, nbo * BLOCK // LANES, width // BLOCK
    place = lambda row, col: (col // 2, row % 2, row // 2)
    chips = [(x, y, z) for z in range(nrow // 2) for y in range(2) for x in range(ncol // 2)]
    tiles = []
    for g in range(nsub):
        for k in range(ncol):
            for t in range(per):
                for c in range(2):
                    l = g % ncol
                    h = l % 2 + 2 * c
                    base = (g - h) % nsub
                    first = (base * blocks * nbo // nbr + nbo - REACH) // 2 % ntile
                    j = (k * per + t - first) % ntile
                    if late * c <= j < span:
                        tiles.append((g // ncol, k, l, t, h, j, base // ncol, base % ncol + l % 2))
    load, choices, chosen = collections.Counter(), [], []
    for row, k, l, t, h, j, to_row, to_col in tiles:
        a, b = place(row, k), place(to_row, to_col)
        ways = [(None, legs(a, b))]
        for q in chips:
            if a != b and q != a and q != b and len(legs(a, q)) + len(legs(q, b)) <= 6:
                ways.append((q, legs(a, q) + legs(q, b)))
        choices.append(ways)
        chosen.append(0)
        load.update(ways[0][1])
    for _ in range(12):
        for i, ways in enumerate(choices):
            load.subtract(ways[chosen[i]][1])
            costs = [
                (sum((load[e] + 1) ** 6 - load[e] ** 6 for e in way) + (0 if q is None else 729), n != chosen[i], n)
                for n, (q, way) in enumerate(ways)
            ]
            chosen[i] = min(costs)[2]
            load.update(ways[chosen[i]][1])
    sends = collections.defaultdict(list)
    relays = collections.defaultdict(list)
    used = collections.Counter()
    order = sorted(range(len(tiles)), key=lambda i: (chosen[i] == 0, tiles[i][5], tiles[i][4], i))
    for i in order:
        row, k, l, t, h, j, to_row, to_col = tiles[i]
        q = choices[i][chosen[i]][0]
        if q is None:
            sends[row, k].append((l, t, h, j, to_row, to_col, None))
        else:
            via_row, via_col = q[2] * 2 + q[1], q[0] * 2 + used[q] % 2
            used[q] += 1
            slot = len(relays[via_row, via_col])
            sends[row, k].append((l, t, h, j, via_row, via_col, slot))
            relays[via_row, via_col].append((h, j, to_row, to_col))
    peers = collections.defaultdict(set)
    for row in range(nrow):
        for k in range(0, ncol, 2):
            peers[row, k].add((row, k + 1))
            peers[row, k + 1].add((row, k))
    for a in list(sends):
        for move in sends[a]:
            if move[4:6] != a:
                peers[a].add(move[4:6])
                peers[move[4:6]].add(a)
    for a in list(relays):
        for move in relays[a]:
            peers[a].add(move[2:4])
            peers[move[2:4]].add(a)
    return sends, relays, peers


def kernel(
    nrow, ncol, nbr, nbo, plan, coeffs_ref, pattern_ref, out_ref, stage, recv, hold, left, right,
    load_sem, send_sem, recv_sem, pass_sem, via_sem, hold_sem,
):
    r, k = lax.axis_index("row"), lax.axis_index("col")
    core = k % 2
    nsub = nrow * ncol
    width = stage.shape[2]
    per = coeffs_ref.shape[1] // LANES
    ntile = nbo * BLOCK // LANES
    span = recv.shape[1]
    blocks = width // BLOCK
    late = 1 if blocks * nbo == nbr else 0

    def first_tile(g):
        center = g * blocks * nbo // nbr
        return (center + nbo - REACH) // 2 % ntile

    loads = lambda l, t: pltpu.make_async_copy(
        coeffs_ref.at[pl.ds(l * width, width), pl.ds(t * LANES, LANES)], stage.at[l, t], load_sem.at[l, t]
    )
    for l in range(ncol):
        for t in range(per):
            loads(l, t).start()

    barrier = pltpu.get_barrier_semaphore()
    me = r * ncol + k
    if plan is None:
        up, down = (r + 1) % nrow, (r + nrow - 1) % nrow
        for d in range(1, ncol):
            pl.semaphore_signal(barrier, inc=1, device_id=(r, (k + d) % ncol), device_id_type=MESH)
        for d in range(ncol):
            pl.semaphore_signal(barrier, inc=1, device_id=(up, (k + d) % ncol), device_id_type=MESH)
            pl.semaphore_signal(barrier, inc=1, device_id=(down, (k + d) % ncol), device_id_type=MESH)
    else:
        sends, relays, peers = plan
        for row, col in sorted(peers):

            @pl.when(me == row * ncol + col)
            def _(others=sorted(peers[row, col])):
                for other in others:
                    pl.semaphore_signal(barrier, inc=1, device_id=other, device_id_type=MESH)

    lane = lax.broadcasted_iota(jnp.int32, (1, LANES), 1)

    def mask(l, t):
        for b in range(blocks):
            p0 = pattern_ref[2 * t, l * blocks + b].astype(jnp.float32)
            p1 = pattern_ref[2 * t + 1, l * blocks + b].astype(jnp.float32)
            rows = pl.ds(b * BLOCK, BLOCK)
            stage[l, t, rows, :] = stage[l, t, rows, :] * jnp.where(lane < BLOCK, p0, p1)

    def target(l, t, c):
        h = l % 2 + 2 * c
        base = (r * ncol + l - h + nsub) % nsub
        j = (k * per + t - first_tile(base) + ntile) % ntile
        wanted = jnp.logical_and(j < span, j >= late * c)
        row, col = base // ncol, base % ncol + l % 2
        here = jnp.logical_and(row == r, col == k)
        j = jnp.minimum(j, span - 1)
        return h, j, row, col, jnp.logical_and(wanted, here), jnp.logical_and(wanted, jnp.logical_not(here))

    def send(l, t, c):
        h, j, row, col, local, remote = target(l, t, c)
        move = pltpu.make_async_remote_copy(
            stage.at[l, t], recv.at[h, j], send_sem.at[l, t, c], recv_sem.at[h, j],
            device_id=(row, col), device_id_type=MESH,
        )
        return local, remote, pltpu.make_async_copy(stage.at[l, t], recv.at[h, j], recv_sem.at[h, j]), move

    def mask_all(l, carry):
        for t in range(per):
            loads(l, t).wait()
            mask(l, t)
        return carry

    lax.fori_loop(0, ncol, mask_all, 0)
    if plan is None:
        pl.semaphore_wait(barrier, 3 * ncol - 1)

    def send_all(l, carry):
        for t in range(per):
            for c in range(2):
                local, remote, own, move = send(l, t, c)
                pl.when(local)(own.start)
                pl.when(remote)(move.start)
        return carry

    def routed(row, col, n):
        l, t, h, j, to_row, to_col, slot = sends[row, col][n]
        if (to_row, to_col) == (row, col):
            return pltpu.make_async_copy(stage.at[l, t], recv.at[h, j], recv_sem.at[h, j])
        return pltpu.make_async_remote_copy(
            stage.at[l, t], recv.at[h, j] if slot is None else hold.at[slot], send_sem.at[l, t, h // 2],
            recv_sem.at[h, j] if slot is None else hold_sem.at[slot],
            device_id=(to_row, to_col), device_id_type=MESH,
        )

    def relayed(row, col, slot):
        h, j, to_row, to_col = relays[row, col][slot]
        return pltpu.make_async_remote_copy(
            hold.at[slot], recv.at[h, j], via_sem.at[slot], recv_sem.at[h, j],
            device_id=(to_row, to_col), device_id_type=MESH,
        )

    def taken(slot):
        return pltpu.make_async_remote_copy(
            hold.at[slot], hold.at[slot], via_sem.at[slot], hold_sem.at[slot],
            device_id=(r, k + 1 - 2 * core), device_id_type=MESH,
        )

    if plan is None:
        lax.fori_loop(0, ncol, send_all, 0)
    else:
        for row, col in sorted(peers):

            @pl.when(me == row * ncol + col)
            def _(row=row, col=col):
                pl.semaphore_wait(barrier, len(peers[row, col]))
                for n in range(len(sends.get((row, col), ()))):
                    routed(row, col, n).start()

    out_ref[...] = jnp.zeros_like(out_ref)
    if plan is not None:
        for row, col in sorted(relays):

            @pl.when(me == row * ncol + col)
            def _(row=row, col=col):
                for slot in range(len(relays[row, col])):
                    taken(slot).wait_recv()
                    relayed(row, col, slot).start()


    def pass_on(h, j):
        return pltpu.make_async_remote_copy(
            recv.at[h, j], recv.at[h, j], pass_sem.at[j], recv_sem.at[h, j],
            device_id=(r, k + 1 - 2 * core), device_id_type=MESH,
        )

    shared, alone = 2 - core, 3 * core

    def arrived(h, j):
        pl.when(j >= jnp.where(h < 2, 0, late))(pass_on(h, j).wait_recv)

    def multiply(j, carry):
        has_shared = j >= jnp.where(shared < 2, 0, late)
        arrived(shared, j)
        pl.when(has_shared)(pass_on(shared, j).start)
        arrived(alone, j)
        arrived(1 + core, j)
        for step in range(STEPS):
            h = core + step

            @pl.when(j >= jnp.where(h < 2, 0, late))
            def _():
                x = recv[h, j]
                high = x.astype(jnp.bfloat16)
                low = (x - high.astype(jnp.float32)).astype(jnp.bfloat16)
                if step == 0:
                    left[:, 0:LANES] = high
                    left[:, LANES:2 * LANES] = low
                    left[:, 2 * LANES:3 * LANES] = high
                right[:, 0:LANES] = high
                right[:, LANES:2 * LANES] = high
                right[:, 2 * LANES:3 * LANES] = low

                for i in range(2):
                    cols = pl.ds(i * (width // 2), width // 2)
                    out_ref[0, step, :, cols] += lax.dot_general(
                        left[...], right[cols, :], (((1,), (1,)), ((), ())),
                        preferred_element_type=jnp.float32,
                    )

        return carry

    lax.fori_loop(0, span, multiply, 0)

    def sent_all(l, carry):
        for t in range(per):
            for c in range(2):
                _, remote, _, move = send(l, t, c)
                pl.when(remote)(move.wait_send)
        return carry

    if plan is None:
        lax.fori_loop(0, ncol, sent_all, 0)
    else:
        for row, col in sorted(peers):

            @pl.when(me == row * ncol + col)
            def _(row=row, col=col):
                for n, move in enumerate(sends.get((row, col), ())):
                    if move[4:6] != (row, col):
                        routed(row, col, n).wait_send()
                for slot in range(len(relays.get((row, col), ()))):
                    relayed(row, col, slot).wait_send()


    def passed_all(j, carry):
        pl.when(j >= jnp.where(shared < 2, 0, late))(pass_on(shared, j).wait_send)
        return carry

    lax.fori_loop(0, span, passed_all, 0)


def shards(nrow, ncol, coeffs, pattern):
    rows, cols = coeffs.shape
    width = rows // ncol
    nbr, nbo = pattern.shape[0] * nrow, pattern.shape[1] * ncol
    per = cols // LANES
    span = REACH + 1
    plan, held = None, 1
    if (nrow, ncol) == (8, 4):
        plan = planned(nrow, ncol, per, width, nbr, nbo, span, 1 if width // BLOCK * nbo == nbr else 0)
        held = max([1] + [len(moves) for moves in plan[1].values()])
    return pl.pallas_call(
        functools.partial(kernel, nrow, ncol, nbr, nbo, plan),
        out_shape=jax.ShapeDtypeStruct((1, STEPS, width, width), jnp.float32),
        in_specs=[pl.BlockSpec(memory_space=pltpu.HBM), pl.BlockSpec(memory_space=pltpu.SMEM)],
        out_specs=pl.BlockSpec(memory_space=pltpu.VMEM),
        scratch_shapes=[
            pltpu.VMEM((ncol, per, width, LANES), jnp.float32),
            pltpu.VMEM((4, span, width, LANES), jnp.float32),
            pltpu.VMEM((held, width, LANES), jnp.float32),
            pltpu.VMEM((width, 3 * LANES), jnp.bfloat16),
            pltpu.VMEM((width, 3 * LANES), jnp.bfloat16),
            pltpu.SemaphoreType.DMA((ncol, per)),
            pltpu.SemaphoreType.DMA((ncol, per, 2)),
            pltpu.SemaphoreType.DMA((4, span)),
            pltpu.SemaphoreType.DMA((span,)),
            pltpu.SemaphoreType.DMA((held,)),
            pltpu.SemaphoreType.DMA((held,)),
        ],
        compiler_params=pltpu.CompilerParams(
            collective_id=0, has_side_effects=True, vmem_limit_bytes=40 << 20
        ),
        cost_estimate=pl.CostEstimate(
            flops=2 * 3 * STEPS * width * width * span * LANES,
            bytes_accessed=4 * (rows * cols + STEPS * width * width), transcendentals=0,
        ),
    )(coeffs, pattern.T)


def solution(mesh):
    in_specs = (P("row", "col"), P("row", "col"))
    out_specs = P(("row", "col"), None, None, None)
    body = functools.partial(shards, mesh.shape["row"], mesh.shape["col"])
    return jax.shard_map(body, mesh=mesh, in_specs=in_specs, out_specs=out_specs, check_vma=False)
```
